32 devices in a mesh: cfg: 2 (over y), seq: 4 (over z), tp: 4 (over x, core).
Axes of the slice: x: 2, y: 2, z: 4, core: 2. Of those that a mesh axis runs over, the one named last changes fastest.
Arguments:
- hidden_in: bfloat16 [2, 4, 1536, 3072], P('cfg', None, 'seq', 'tp'), as said below
- w_qkv: bfloat16 [3072, 3, 3072], P(None, None, 'tp')
- w_mlp: bfloat16 [3072, 6144], P(None, 'tp'), may hold values from -0.109375 to 0.109375
- w_attn_out: bfloat16 [3072, 3072], P('tp'), may hold values from -0.109375 to 0.109375
- w_mlp_out: bfloat16 [6144, 3072], P('tp'), may hold values from -0.0625 to 0.0625
- mod_table: float32 [28, 3, 3072], replicated, may hold values from -6 to 6
- qk_gain: float32 [2, 128], replicated, as said below
- timestep: int32 [4], replicated, may hold values from 0 to 27
- text_len: int32 [2, 4], P('cfg'), may hold values from 128 to 512
- pos_ids: int32 [4, 3, 1536], P(None, None, 'seq'), may hold values from 0 to 158, as said below
Outputs:
- guided: bfloat16 [4, 1536, 3072], P('cfg', 'seq', 'tp')
- state_norm: float32 [2, 4], P('cfg')
- max_logit: float32 [2, 4], P('cfg')
The draws below stay inside these ranges and needn't reach their ends.
Inputs may be any that keep to these rules, and one draw needn't show every extreme that they name: `hidden_in`: the entries have scales that differ between tokens and between features. `qk_gain`: positive gains. `pos_ids`: text tokens have ids 0 on all axes; image token i of a request (token 512 + i) has ids 0, i // 32 + a and i % 32 + b, with offsets a and b of the request in 0 to 127; one request has both offsets 4 * 32 - 1.
All inputs are finite; a program needn't handle non-finite values.
Results may differ from the reference program's by a relative error of at most 0.0025.
Values may be sent and summed in bfloat16 or wider, within the bound.
A program may use at most 192 MiB of HBM per device.

```python
import math
import jax
import jax.numpy as jnp
from jax import lax

D = 3072
HEADS = 24
HD = 128
FF = 6144
TXT = 512
GRID = 32
STEPS = 28
REQ = 4
SEQ_LEN = 1536
INNER = 3072


def draw_hidden_in(key, part):
    key_base, key_rows, key_cols = jax.random.split(key, 3)
    shape = (2, REQ, SEQ_LEN, D)
    position = jnp.arange(SEQ_LEN, dtype=jnp.int32)
    rising = jnp.power(3.0, position.astype(jnp.float32) / SEQ_LEN)[None, None, :, None]
    col_scale = jnp.exp(jax.random.uniform(key_cols, (1, 1, 1, D), jnp.float32, 0.0, math.log(3.0)))
    base_draw = jax.random.normal(key_base, shape, jnp.float32)
    row_scale = jnp.exp(jax.random.uniform(key_rows, (2, REQ, SEQ_LEN, 1), jnp.float32, 0.0, math.log(3.0)))
    values = base_draw * row_scale * rising * col_scale
    return values.astype(jnp.bfloat16)


def draw_w_qkv(key, part):
    key_base = jax.random.fold_in(key, 0)
    base_draw = jax.random.normal(key_base, (D, 3, INNER), jnp.float32) / math.sqrt(D)
    return base_draw.astype(jnp.bfloat16)


def draw_qk_gain(key, part):
    return jnp.exp(jax.random.uniform(key, (2, HD), jnp.float32, math.log(1.2), math.log(2.4)))


def draw_pos_ids(key, part):
    key_offsets, key_chosen = jax.random.split(key, 2)
    offsets = jax.random.randint(key_offsets, (REQ, 2), 0, 4 * GRID)
    chosen = jax.random.randint(key_chosen, (), 0, REQ)
    is_chosen = jnp.arange(REQ, dtype=jnp.int32)[:, None] == chosen
    offsets = jnp.where(is_chosen, 4 * GRID - 1, offsets).astype(jnp.int32)
    image_index = jnp.arange(SEQ_LEN, dtype=jnp.int32) - TXT
    is_image = image_index >= 0
    safe_index = jnp.maximum(image_index, 0)
    row_ids = jnp.where(is_image[None, :], safe_index[None, :] // GRID + offsets[:, 0:1], 0)
    col_ids = jnp.where(is_image[None, :], safe_index[None, :] % GRID + offsets[:, 1:2], 0)
    zero_ids = jnp.zeros((REQ, SEQ_LEN), jnp.int32)
    return jnp.stack([zero_ids, row_ids, col_ids], axis=1).astype(jnp.int32)


def set_ends(array, own_key, least, high):
    extent = array.shape
    index_at = [jax.random.randint(jax.random.fold_in(own_key, axis), (), 0, extent[axis]) for axis in range(len(extent))]
    array = array.at[tuple(index_at)].set(least)
    longest = extent.index(max(extent))
    index_at[longest] = (index_at[longest] + 1) % extent[longest]
    return array.at[tuple(index_at)].set(high)


def levels(own_key, extent, shards, smallest, largest):
    def one(dim, shards_of):
        draws = jax.random.uniform(jax.random.fold_in(jax.random.fold_in(own_key, 6), dim), (shards_of,), jnp.float32, smallest / len(shards), largest / len(shards))
        return jnp.repeat(jnp.exp(draws), extent[dim] // shards_of).reshape((-1,) + (1,) * (len(extent) - dim - 1))

    loudness = one(*shards[0])
    for cut in shards[1:]:
        loudness = loudness * one(*cut)
    return loudness


def noise(stream_key, extent, deviation, most, cuts=(), held_as=jnp.bfloat16):
    result = deviation * jax.random.normal(stream_key, extent, jnp.float32)
    if cuts:
        result = result * levels(stream_key, extent, cuts, -0.22, 0.18)
    return jnp.clip(result, -most, most).astype(held_as)


def setup_inputs(seed: int = 0) -> dict:
    key_list = jax.random.split(jax.random.key(seed), 11)
    hidden_in = draw_hidden_in(jax.random.fold_in(key_list[10], 71), 0)
    w_qkv = draw_w_qkv(jax.random.fold_in(key_list[10], 71), 0)
    w_mlp = noise(key_list[2], (D, FF), D ** -0.5, 0.109375, ((1, 4),))
    w_attn_out = noise(key_list[3], (INNER, D), INNER ** -0.5, 0.109375, ((0, 4),))
    w_mlp_out = noise(key_list[4], (FF, D), (INNER + FF) ** -0.5, 0.0625, ((0, 4),))
    mod_table = noise(key_list[5], (STEPS, 3, D), 1.0, 6.0, (), jnp.float32)
    qk_gain = draw_qk_gain(jax.random.fold_in(key_list[10], 71), 0)
    timestep = set_ends(jax.random.randint(key_list[7], (REQ,), 0, STEPS), jax.random.fold_in(key_list[7], 1), 0, STEPS - 1).astype(jnp.int32)
    text_len = set_ends(jax.random.randint(key_list[8], (2, REQ), TXT // 4, TXT + 1), jax.random.fold_in(key_list[8], 1), TXT // 4, TXT).astype(jnp.int32)
    pos_ids = draw_pos_ids(jax.random.fold_in(key_list[10], 71), 0)
    return dict(hidden_in=hidden_in, w_qkv=w_qkv, w_mlp=w_mlp, w_attn_out=w_attn_out, w_mlp_out=w_mlp_out, mod_table=mod_table, qk_gain=qk_gain, timestep=timestep, text_len=text_len, pos_ids=pos_ids)


norm_eps = 1e-06
rope_theta = 10000.0
guidance_scale = 4.0
rescale_share = 0.7
masked_value = -1e+30

def lookup_rows(mod_table, timestep):
    step_count = mod_table.shape[0]
    onehot = timestep[:, None] == jnp.arange(step_count, dtype=jnp.int32)[None, :]
    return lax.optimization_barrier(jnp.sum(jnp.where(onehot[:, :, None, None], mod_table[None], jnp.float32(0.0)), axis=1))

def rope_tables(pos_ids, head_size):
    pair_index = jnp.arange(head_size, dtype=jnp.int32) // 2
    first_end = head_size // 16
    second = first_end + (head_size - head_size // 8) // 4
    axis_of = jnp.where(pair_index < first_end, 0, jnp.where(pair_index < second, 1, 2))
    offset = pair_index - jnp.where(axis_of == 0, 0, jnp.where(axis_of == 1, first_end, second))
    pair_span = jnp.where(axis_of == 0, head_size // 8, (head_size - head_size // 8) // 2)
    frequency = jnp.power(jnp.float32(rope_theta), -2.0 * offset.astype(jnp.float32) / pair_span.astype(jnp.float32))
    angles = jnp.zeros((pos_ids.shape[0], pos_ids.shape[2], head_size), jnp.float32)
    for axis_id in range(3):
        column = jnp.where(axis_of == axis_id, frequency, jnp.float32(0.0))
        angles = angles + pos_ids[:, axis_id, :, None].astype(jnp.float32) * column[None, None, :]
    row_ids = jnp.arange(head_size, dtype=jnp.int32)[:, None]
    col_ids = jnp.arange(head_size, dtype=jnp.int32)[None, :]
    swapper = jnp.where((col_ids % 2 == 0) & (row_ids == col_ids + 1), -1.0, jnp.where((col_ids % 2 == 1) & (row_ids == col_ids - 1), 1.0, 0.0)).astype(jnp.float32)
    return (jnp.cos(angles), jnp.sin(angles), swapper)

def head_norm(values, gain_row):
    return values * lax.rsqrt(lax.optimization_barrier(jnp.mean(values * values, axis=-1, keepdims=True)) + norm_eps) * gain_row

def rotate(values, cosine, sine_table, swapper):
    turned = jnp.einsum('rshd,de->rshe', values, swapper, precision=lax.Precision.HIGHEST)
    return values * cosine[:, :, None, :] + turned * sine_table[:, :, None, :]

def modulate(tokens, modulation):
    values = tokens.astype(jnp.float32)
    center = values - lax.optimization_barrier(jnp.mean(values, axis=-1, keepdims=True))
    normed = center * lax.rsqrt(lax.optimization_barrier(jnp.mean(center * center, axis=-1, keepdims=True)) + norm_eps)
    return ((1.0 + modulation[:, 1, None, :]) * normed + modulation[:, 0, None, :]).astype(jnp.bfloat16)

def reference(hidden_in, w_qkv, w_mlp, w_attn_out, w_mlp_out, mod_table, qk_gain, timestep, text_len, pos_ids):
    modulation = lookup_rows(mod_table, timestep)
    cosine, sine_table, swapper = rope_tables(pos_ids, HD)
    positions = jnp.arange(SEQ_LEN, dtype=jnp.int32)
    score_scale = HD ** (-0.5)
    new_states = []
    peak_list = []
    for copy_id in range(2):
        tokens = hidden_in[copy_id]
        modded = modulate(tokens, modulation)
        flat_rows = modded.reshape(REQ * SEQ_LEN, D)
        projected = jnp.dot(flat_rows, w_qkv.reshape(D, 3 * INNER), preferred_element_type=jnp.float32)
        projected = projected.reshape(REQ, SEQ_LEN, 3, HEADS, HD)
        queries = rotate(head_norm(projected[:, :, 0], qk_gain[0]), cosine, sine_table, swapper).astype(jnp.bfloat16)
        key_all = rotate(head_norm(projected[:, :, 1], qk_gain[1]), cosine, sine_table, swapper).astype(jnp.bfloat16)
        value_all = projected[:, :, 2].astype(jnp.bfloat16)
        usable = (positions[None, :] >= TXT) | (positions[None, :] < text_len[copy_id][:, None])

        def attend_head(operands):
            query_head, key_head, value_head = operands
            scores = jnp.einsum('rqd,rkd->rqk', query_head.astype(jnp.float32), key_head.astype(jnp.float32)) * score_scale
            scores = jnp.where(usable[:, None, :], scores, masked_value)
            row_peak = lax.optimization_barrier(jnp.max(scores, axis=-1))
            weights = jnp.where(usable[:, None, :], jnp.exp(scores - row_peak[..., None]), 0.0)
            weight_sum = lax.optimization_barrier(jnp.sum(weights, axis=-1))
            rounded = lax.optimization_barrier(weights.astype(jnp.bfloat16))
            mixture = jnp.einsum('rqk,rkd->rqd', rounded.astype(jnp.float32), value_head.astype(jnp.float32))
            return (mixture / weight_sum[..., None], lax.optimization_barrier(jnp.max(row_peak, axis=-1)))
        mixture, head_peaks = lax.map(attend_head, (jnp.transpose(queries, (2, 0, 1, 3)), jnp.transpose(key_all, (2, 0, 1, 3)), jnp.transpose(value_all, (2, 0, 1, 3))))
        attended = jnp.transpose(mixture, (1, 2, 0, 3)).reshape(REQ * SEQ_LEN, INNER).astype(jnp.bfloat16)
        hidden_units = jax.nn.gelu(jnp.dot(flat_rows, w_mlp, preferred_element_type=jnp.float32), approximate=True).astype(jnp.bfloat16)
        branch = jnp.dot(attended, w_attn_out, preferred_element_type=jnp.float32) + jnp.dot(hidden_units, w_mlp_out, preferred_element_type=jnp.float32)
        new_state = tokens.astype(jnp.float32) + modulation[:, 2, None, :] * branch.reshape(REQ, SEQ_LEN, D)
        new_states.append(new_state)
        peak_list.append(lax.optimization_barrier(jnp.max(head_peaks, axis=0)))
    entries = float(SEQ_LEN * D)
    conditional = new_states[0]
    unconditional = new_states[1]
    raw = unconditional + guidance_scale * (conditional - unconditional)
    norms = [jnp.sqrt(lax.optimization_barrier(jnp.sum(one * one, axis=(1, 2))) / entries + norm_eps) for one in new_states]
    raw_norm = jnp.sqrt(lax.optimization_barrier(jnp.sum(raw * raw, axis=(1, 2))) / entries + norm_eps)
    factor = rescale_share * norms[0] / raw_norm + (1.0 - rescale_share)
    guided = (raw * factor[:, None, None]).astype(jnp.bfloat16)
    return (guided, jnp.stack(norms, axis=0), jnp.stack(peak_list, axis=0))
```

```python
import jax
import jax.numpy as jnp
from jax import lax
from jax.sharding import PartitionSpec as P

D = 3072
TXT = 512
SEQ_LEN = 1536
REQUESTS = 4


norm_eps = 1e-06
rope_theta = 10000.0
guidance_scale = 4.0
rescale_share = 0.7
masked_value = -1e30


def lookup_rows(mod_table, timestep):
    step_count = mod_table.shape[0]
    onehot = timestep[:, None] == jnp.arange(step_count, dtype=jnp.int32)[None, :]
    return jnp.sum(jnp.where(onehot[:, :, None, None], mod_table[None], jnp.float32(0.0)), axis=1)


def rope_tables(pos_ids, head_size):
    pair_index = jnp.arange(head_size, dtype=jnp.int32) // 2
    first_end = head_size // 16
    second = first_end + (head_size - head_size // 8) // 4
    axis_of = jnp.where(pair_index < first_end, 0, jnp.where(pair_index < second, 1, 2))
    offset = pair_index - jnp.where(axis_of == 0, 0, jnp.where(axis_of == 1, first_end, second))
    pair_span = jnp.where(axis_of == 0, head_size // 8, (head_size - head_size // 8) // 2)
    frequency = jnp.power(
        jnp.float32(rope_theta), -2.0 * offset.astype(jnp.float32) / pair_span.astype(jnp.float32)
    )
    angles = jnp.zeros((pos_ids.shape[0], pos_ids.shape[2], head_size), jnp.float32)
    for axis_id in range(3):
        column = jnp.where(axis_of == axis_id, frequency, jnp.float32(0.0))
        angles = angles + pos_ids[:, axis_id, :, None].astype(jnp.float32) * column[None, None, :]
    row_ids = jnp.arange(head_size, dtype=jnp.int32)[:, None]
    col_ids = jnp.arange(head_size, dtype=jnp.int32)[None, :]
    swapper = jnp.where(
        (col_ids % 2 == 0) & (row_ids == col_ids + 1),
        -1.0,
        jnp.where((col_ids % 2 == 1) & (row_ids == col_ids - 1), 1.0, 0.0),
    ).astype(jnp.float32)
    return (jnp.cos(angles), jnp.sin(angles), swapper)


def head_norm(values, gain_row):
    return (
        values * lax.rsqrt(jnp.mean(values * values, axis=-1, keepdims=True) + norm_eps) * gain_row
    )


def rotate(values, cosine, sine_table, swapper):
    turned = jnp.einsum("rshd,de->rshe", values, swapper, precision=lax.Precision.HIGHEST)
    return values * cosine[:, :, None, :] + turned * sine_table[:, :, None, :]


def modulate(tokens, modulation):
    values = tokens.astype(jnp.float32)
    center = values - jnp.mean(values, axis=-1, keepdims=True)
    normed = center * lax.rsqrt(jnp.mean(center * center, axis=-1, keepdims=True) + norm_eps)
    return ((1.0 + modulation[:, 1, None, :]) * normed + modulation[:, 0, None, :]).astype(
        jnp.bfloat16
    )


def local(
    hidden_in, w_qkv, w_mlp, w_attn_out, w_mlp_out, mod_table, qk_gain, timestep, text_len, pos_ids
):
    tokens = hidden_in[0]
    requests, local_len, local_width = tokens.shape
    head_size = qk_gain.shape[1]
    local_inner = w_qkv.shape[2]
    local_heads = local_inner // head_size
    full_tokens = lax.all_gather(tokens, "tp", axis=2, tiled=True)
    model_width = full_tokens.shape[2]
    modulation = lookup_rows(mod_table, timestep)
    modded = modulate(full_tokens, modulation)
    flat_rows = modded.reshape(requests * local_len, model_width)
    projected = jnp.dot(
        flat_rows, w_qkv.reshape(model_width, 3 * local_inner), preferred_element_type=jnp.float32
    )
    projected = projected.reshape(requests, local_len, 3, local_heads, head_size)
    cosine, sine_table, swapper = rope_tables(pos_ids, head_size)
    queries = rotate(head_norm(projected[:, :, 0], qk_gain[0]), cosine, sine_table, swapper).astype(
        jnp.bfloat16
    )
    key_local = rotate(
        head_norm(projected[:, :, 1], qk_gain[1]), cosine, sine_table, swapper
    ).astype(jnp.bfloat16)
    key_local = key_local.reshape(requests, local_len, local_inner)
    value_local = projected[:, :, 2].astype(jnp.bfloat16).reshape(requests, local_len, local_inner)
    lengths = text_len[0]
    score_scale = head_size ** (-0.5)
    key_rows, value_rows = (
        lax.all_gather(key_local, "seq", axis=1, tiled=True),
        lax.all_gather(value_local, "seq", axis=1, tiled=True),
    )
    total_len = key_rows.shape[1]
    key_heads = key_rows.reshape(requests, total_len, local_heads, head_size)
    value_heads = value_rows.reshape(requests, total_len, local_heads, head_size)
    scores = (
        jnp.einsum("rqhd,rkhd->rhqk", queries, key_heads, preferred_element_type=jnp.float32)
        * score_scale
    )
    positions = jnp.arange(total_len, dtype=jnp.int32)
    usable = (positions[None, :] >= TXT) | (positions[None, :] < lengths[:, None])
    scores = jnp.where(usable[:, None, None, :], scores, masked_value)
    row_peak = jnp.max(scores, axis=-1)
    weights = jnp.where(usable[:, None, None, :], jnp.exp(scores - row_peak[..., None]), 0.0)
    weight_sum = jnp.sum(weights, axis=-1)
    mixture = jnp.einsum(
        "rhqk,rkhd->rqhd",
        weights.astype(jnp.bfloat16),
        value_heads,
        preferred_element_type=jnp.float32,
    )
    mixture = mixture / jnp.transpose(weight_sum, (0, 2, 1))[..., None]
    peak_logit = jnp.max(row_peak, axis=(1, 2))
    attended = mixture.reshape(requests * local_len, local_inner).astype(jnp.bfloat16)
    hidden_units = jax.nn.gelu(
        jnp.dot(flat_rows, w_mlp, preferred_element_type=jnp.float32), approximate=True
    ).astype(jnp.bfloat16)
    partial_out = jnp.dot(attended, w_attn_out, preferred_element_type=jnp.float32) + jnp.dot(
        hidden_units, w_mlp_out, preferred_element_type=jnp.float32
    )
    partial_out = partial_out.reshape(requests, local_len, model_width)
    branch = lax.psum_scatter(partial_out, "tp", scatter_dimension=2, tiled=True)
    gate_rows = lax.dynamic_slice_in_dim(
        modulation[:, 2, :], lax.axis_index("tp") * local_width, local_width, 1
    )
    new_state = tokens.astype(jnp.float32) + gate_rows[:, None, :] * branch
    peak_logit = lax.pmax(peak_logit, ("seq", "tp"))
    own_local = jnp.sum(new_state * new_state, axis=(1, 2))
    half_req = requests // 2
    paired = lax.all_to_all(
        new_state.reshape(2, half_req, local_len, local_width),
        "cfg",
        split_axis=0,
        concat_axis=0,
        tiled=True,
    )
    conditional = paired[0]
    unconditional = paired[1]
    raw = unconditional + guidance_scale * (conditional - unconditional)
    entries = float(SEQ_LEN * D)
    own_square = lax.psum(own_local, ("seq", "tp"))
    raw_square, cond_square = lax.psum(
        (jnp.sum(raw * raw, axis=(1, 2)), jnp.sum(conditional * conditional, axis=(1, 2))),
        ("seq", "tp"),
    )
    state_norm = jnp.sqrt(own_square / entries + norm_eps)
    factor = rescale_share * jnp.sqrt(cond_square / entries + norm_eps) / jnp.sqrt(
        raw_square / entries + norm_eps
    ) + (1.0 - rescale_share)
    guided = (raw * factor[:, None, None]).astype(jnp.bfloat16)
    return (guided, state_norm[None, :], peak_logit[None, :])


CHUNKS_IN = 2
CHUNKS_OUT = 2


def local_by_request(
    hidden_in, w_qkv, w_mlp, w_attn_out, w_mlp_out, mod_table, qk_gain, timestep, text_len, pos_ids
):
    tokens = hidden_in[0]
    requests, local_len, local_width = tokens.shape
    head_size = qk_gain.shape[1]
    local_inner = w_qkv.shape[2]
    local_heads = local_inner // head_size
    seq_size = lax.axis_size("seq")
    total_len = local_len * seq_size
    half_req = requests // 2
    my_request = lax.axis_index("seq")
    my_copy = lax.axis_index("cfg")
    modulation = lookup_rows(mod_table, timestep)
    own_mod = lax.dynamic_slice_in_dim(modulation, my_request, 1, 0)

    step_in = local_len // CHUNKS_IN
    w_flat = w_qkv.reshape(w_qkv.shape[0], 3 * local_inner)
    pos_mine = lax.all_to_all(pos_ids, "seq", split_axis=0, concat_axis=0, tiled=True)
    modded_parts = []
    for c in range(CHUNKS_IN):
        piece = lax.slice_in_dim(tokens, c * step_in, (c + 1) * step_in, axis=1)
        got = lax.all_to_all(piece, "seq", split_axis=0, concat_axis=0, tiled=True)
        rows = got.reshape(seq_size * step_in, local_width)
        full = lax.all_gather(rows, "tp", axis=1, tiled=True)
        modded_parts.append(modulate(full[None], own_mod)[0])
    halves = tokens.reshape(2, half_req, local_len, local_width)
    swapped = lax.all_to_all(halves, "cfg", split_axis=0, concat_axis=0, tiled=True)

    positions = (
        jnp.arange(seq_size, dtype=jnp.int32)[None, :, None] * local_len
        + jnp.arange(CHUNKS_IN, dtype=jnp.int32)[:, None, None] * step_in
        + jnp.arange(step_in, dtype=jnp.int32)[None, None, :]
    ).reshape(total_len)
    ids = pos_mine.reshape(seq_size, 3, CHUNKS_IN, step_in)
    ids = jnp.transpose(ids, (1, 2, 0, 3)).reshape(1, 3, total_len)
    cosine, sine_table, swapper = rope_tables(ids, head_size)
    length = lax.dynamic_slice_in_dim(text_len[0], my_request, 1, 0)
    usable = (positions >= TXT) | (positions < length)
    score_scale = head_size ** (-0.5)

    q_parts, k_parts, v_parts, hidden_parts = [], [], [], []
    part_len = seq_size * step_in
    for c in range(CHUNKS_IN):
        projected = jnp.dot(modded_parts[c], w_flat, preferred_element_type=jnp.float32)
        projected = projected.reshape(1, part_len, 3, local_heads, head_size)
        cos_c = lax.slice_in_dim(cosine, c * part_len, (c + 1) * part_len, axis=1)
        sin_c = lax.slice_in_dim(sine_table, c * part_len, (c + 1) * part_len, axis=1)
        q_parts.append(
            rotate(head_norm(projected[:, :, 0], qk_gain[0]), cos_c, sin_c, swapper).astype(
                jnp.bfloat16
            )[0]
        )
        k_parts.append(
            rotate(head_norm(projected[:, :, 1], qk_gain[1]), cos_c, sin_c, swapper).astype(
                jnp.bfloat16
            )[0]
        )
        v_parts.append(projected[0, :, 2].astype(jnp.bfloat16))
        hidden_parts.append(
            jax.nn.gelu(
                jnp.dot(modded_parts[c], w_mlp, preferred_element_type=jnp.float32),
                approximate=True,
            ).astype(jnp.bfloat16)
        )
    queries = jnp.concatenate(q_parts, axis=0)
    keys = jnp.concatenate(k_parts, axis=0)
    values = jnp.concatenate(v_parts, axis=0)
    hidden_units = jnp.concatenate(hidden_parts, axis=0)

    scores = (
        jnp.einsum("qhd,khd->hqk", queries, keys, preferred_element_type=jnp.float32) * score_scale
    )
    scores = jnp.where(usable[None, None, :], scores, masked_value)
    row_peak = jnp.max(scores, axis=-1)
    weights = jnp.where(usable[None, None, :], jnp.exp(scores - row_peak[..., None]), 0.0)
    weight_sum = jnp.sum(weights, axis=-1)
    mixture = jnp.einsum(
        "hqk,khd->qhd", weights.astype(jnp.bfloat16), values, preferred_element_type=jnp.float32
    )
    mixture = mixture / jnp.transpose(weight_sum, (1, 0))[..., None]
    attended = mixture.reshape(total_len, local_inner).astype(jnp.bfloat16)
    peak = jnp.where(jnp.arange(requests) == my_request, jnp.max(row_peak), -jnp.inf)
    peak_logit = lax.pmax(peak, ("seq", "tp"))

    attended = attended.reshape(CHUNKS_IN, seq_size, step_in, local_inner)
    hidden_units = hidden_units.reshape(CHUNKS_IN, seq_size, step_in, -1)
    per = CHUNKS_OUT // CHUNKS_IN
    step_out = step_in // per
    own_parts, other_parts = [], []
    for c in range(CHUNKS_OUT):
        big, small = c // per, c % per
        at = slice(small * step_out, (small + 1) * step_out)
        a_rows = attended[big, :, at].reshape(seq_size * step_out, -1)
        h_rows = hidden_units[big, :, at].reshape(seq_size * step_out, -1)
        partial_out = jnp.dot(a_rows, w_attn_out, preferred_element_type=jnp.float32) + jnp.dot(
            h_rows, w_mlp_out, preferred_element_type=jnp.float32
        )
        summed = lax.psum_scatter(
            partial_out.astype(jnp.bfloat16), "tp", scatter_dimension=1, tiled=True
        )
        back = lax.all_to_all(
            summed.reshape(seq_size, step_out, local_width),
            "seq",
            split_axis=0,
            concat_axis=0,
            tiled=True,
        )
        own_parts.append(back)
        other_parts.append(
            lax.all_to_all(
                back.reshape(2, half_req, step_out, local_width),
                "cfg",
                split_axis=0,
                concat_axis=0,
                tiled=True,
            )
        )
    gate_rows = lax.dynamic_slice_in_dim(
        modulation[:, 2, :], lax.axis_index("tp") * local_width, local_width, 1
    )
    guide_gate = lax.dynamic_slice_in_dim(gate_rows, my_copy * half_req, half_req, 0)
    own_sum = jnp.zeros((requests,), jnp.float32)
    raw_sum = jnp.zeros((half_req,), jnp.float32)
    cond_sum = jnp.zeros((half_req,), jnp.float32)
    raws = []
    for c in range(CHUNKS_OUT):
        at = slice(c * step_out, (c + 1) * step_out)
        own_state = tokens[:, at].astype(jnp.float32) + gate_rows[:, None, :] * own_parts[c].astype(
            jnp.float32
        )
        own_sum = own_sum + jnp.sum(own_state * own_state, axis=(1, 2))
        pair = swapped[:, :, at].astype(jnp.float32) + guide_gate[None, :, None, :] * other_parts[
            c
        ].astype(jnp.float32)
        raw = pair[1] + guidance_scale * (pair[0] - pair[1])
        raw_sum = raw_sum + jnp.sum(raw * raw, axis=(1, 2))
        cond_sum = cond_sum + jnp.sum(pair[0] * pair[0], axis=(1, 2))
        raws.append(raw)
    entries = float(SEQ_LEN * D)
    sums = lax.psum(jnp.concatenate([own_sum, raw_sum, cond_sum]), ("seq", "tp"))
    own_square = sums[:requests]
    raw_square = sums[requests : requests + half_req]
    cond_square = sums[requests + half_req :]
    state_norm = jnp.sqrt(own_square / entries + norm_eps)
    factor = rescale_share * jnp.sqrt(cond_square / entries + norm_eps) / jnp.sqrt(
        raw_square / entries + norm_eps
    ) + (1.0 - rescale_share)
    guided = (jnp.concatenate(raws, axis=1) * factor[:, None, None]).astype(jnp.bfloat16)
    return (guided, state_norm[None, :], peak_logit[None, :])


def solution(mesh):
    placed = (
        P("cfg", None, "seq", "tp"),
        P(None, None, "tp"),
        P(None, "tp"),
        P("tp", None),
        P("tp", None),
        P(),
        P(),
        P(),
        P("cfg", None),
        P(None, None, "seq"),
    )
    body = local_by_request if mesh.shape["seq"] == REQUESTS else local
    return jax.shard_map(
        body,
        mesh=mesh,
        in_specs=placed,
        out_specs=(P("cfg", "seq", "tp"), P("cfg", None), P("cfg", None)),
        check_vma=False,
    )
```

```python
import jax
import jax.numpy as jnp
from jax import lax
from jax.experimental import pallas as pl
from jax.experimental.pallas import tpu as pltpu
from jax.sharding import PartitionSpec as P

D = 3072
TXT = 512
SEQ_LEN = 1536
REQUESTS = 4


norm_eps = 1e-06
rope_theta = 10000.0
guidance_scale = 4.0
rescale_share = 0.7
masked_value = -1e30


def lookup_rows(mod_table, timestep):
    step_count = mod_table.shape[0]
    onehot = timestep[:, None] == jnp.arange(step_count, dtype=jnp.int32)[None, :]
    return jnp.sum(jnp.where(onehot[:, :, None, None], mod_table[None], jnp.float32(0.0)), axis=1)


def rope_tables(pos_ids, head_size):
    pair_index = jnp.arange(head_size, dtype=jnp.int32) // 2
    first_end = head_size // 16
    second = first_end + (head_size - head_size // 8) // 4
    axis_of = jnp.where(pair_index < first_end, 0, jnp.where(pair_index < second, 1, 2))
    offset = pair_index - jnp.where(axis_of == 0, 0, jnp.where(axis_of == 1, first_end, second))
    pair_span = jnp.where(axis_of == 0, head_size // 8, (head_size - head_size // 8) // 2)
    frequency = jnp.power(
        jnp.float32(rope_theta), -2.0 * offset.astype(jnp.float32) / pair_span.astype(jnp.float32)
    )
    angles = jnp.zeros((pos_ids.shape[0], pos_ids.shape[2], head_size), jnp.float32)
    for axis_id in range(3):
        column = jnp.where(axis_of == axis_id, frequency, jnp.float32(0.0))
        angles = angles + pos_ids[:, axis_id, :, None].astype(jnp.float32) * column[None, None, :]
    row_ids = jnp.arange(head_size, dtype=jnp.int32)[:, None]
    col_ids = jnp.arange(head_size, dtype=jnp.int32)[None, :]
    swapper = jnp.where(
        (col_ids % 2 == 0) & (row_ids == col_ids + 1),
        -1.0,
        jnp.where((col_ids % 2 == 1) & (row_ids == col_ids - 1), 1.0, 0.0),
    ).astype(jnp.float32)
    return (jnp.cos(angles), jnp.sin(angles), swapper)


def head_norm(values, gain_row):
    return (
        values * lax.rsqrt(jnp.mean(values * values, axis=-1, keepdims=True) + norm_eps) * gain_row
    )


def rotate(values, cosine, sine_table, swapper):
    turned = jnp.einsum("rshd,de->rshe", values, swapper, precision=lax.Precision.HIGHEST)
    return values * cosine[:, :, None, :] + turned * sine_table[:, :, None, :]


def modulate(tokens, modulation):
    values = tokens.astype(jnp.float32)
    center = values - jnp.mean(values, axis=-1, keepdims=True)
    normed = center * lax.rsqrt(jnp.mean(center * center, axis=-1, keepdims=True) + norm_eps)
    return ((1.0 + modulation[:, 1, None, :]) * normed + modulation[:, 0, None, :]).astype(
        jnp.bfloat16
    )


def local(
    hidden_in, w_qkv, w_mlp, w_attn_out, w_mlp_out, mod_table, qk_gain, timestep, text_len, pos_ids
):
    tokens = hidden_in[0]
    requests, local_len, local_width = tokens.shape
    head_size = qk_gain.shape[1]
    local_inner = w_qkv.shape[2]
    local_heads = local_inner // head_size
    full_tokens = lax.all_gather(tokens, "tp", axis=2, tiled=True)
    model_width = full_tokens.shape[2]
    modulation = lookup_rows(mod_table, timestep)
    modded = modulate(full_tokens, modulation)
    flat_rows = modded.reshape(requests * local_len, model_width)
    projected = jnp.dot(
        flat_rows, w_qkv.reshape(model_width, 3 * local_inner), preferred_element_type=jnp.float32
    )
    projected = projected.reshape(requests, local_len, 3, local_heads, head_size)
    cosine, sine_table, swapper = rope_tables(pos_ids, head_size)
    queries = rotate(head_norm(projected[:, :, 0], qk_gain[0]), cosine, sine_table, swapper).astype(
        jnp.bfloat16
    )
    key_local = rotate(
        head_norm(projected[:, :, 1], qk_gain[1]), cosine, sine_table, swapper
    ).astype(jnp.bfloat16)
    key_local = key_local.reshape(requests, local_len, local_inner)
    value_local = projected[:, :, 2].astype(jnp.bfloat16).reshape(requests, local_len, local_inner)
    lengths = text_len[0]
    score_scale = head_size ** (-0.5)
    key_rows, value_rows = (
        lax.all_gather(key_local, "seq", axis=1, tiled=True),
        lax.all_gather(value_local, "seq", axis=1, tiled=True),
    )
    total_len = key_rows.shape[1]
    key_heads = key_rows.reshape(requests, total_len, local_heads, head_size)
    value_heads = value_rows.reshape(requests, total_len, local_heads, head_size)
    scores = (
        jnp.einsum("rqhd,rkhd->rhqk", queries, key_heads, preferred_element_type=jnp.float32)
        * score_scale
    )
    positions = jnp.arange(total_len, dtype=jnp.int32)
    usable = (positions[None, :] >= TXT) | (positions[None, :] < lengths[:, None])
    scores = jnp.where(usable[:, None, None, :], scores, masked_value)
    row_peak = jnp.max(scores, axis=-1)
    weights = jnp.where(usable[:, None, None, :], jnp.exp(scores - row_peak[..., None]), 0.0)
    weight_sum = jnp.sum(weights, axis=-1)
    mixture = jnp.einsum(
        "rhqk,rkhd->rqhd",
        weights.astype(jnp.bfloat16),
        value_heads,
        preferred_element_type=jnp.float32,
    )
    mixture = mixture / jnp.transpose(weight_sum, (0, 2, 1))[..., None]
    peak_logit = jnp.max(row_peak, axis=(1, 2))
    attended = mixture.reshape(requests * local_len, local_inner).astype(jnp.bfloat16)
    hidden_units = jax.nn.gelu(
        jnp.dot(flat_rows, w_mlp, preferred_element_type=jnp.float32), approximate=True
    ).astype(jnp.bfloat16)
    partial_out = jnp.dot(attended, w_attn_out, preferred_element_type=jnp.float32) + jnp.dot(
        hidden_units, w_mlp_out, preferred_element_type=jnp.float32
    )
    partial_out = partial_out.reshape(requests, local_len, model_width)
    branch = lax.psum_scatter(partial_out, "tp", scatter_dimension=2, tiled=True)
    gate_rows = lax.dynamic_slice_in_dim(
        modulation[:, 2, :], lax.axis_index("tp") * local_width, local_width, 1
    )
    new_state = tokens.astype(jnp.float32) + gate_rows[:, None, :] * branch
    peak_logit = lax.pmax(peak_logit, ("seq", "tp"))
    own_local = jnp.sum(new_state * new_state, axis=(1, 2))
    half_req = requests // 2
    paired = lax.all_to_all(
        new_state.reshape(2, half_req, local_len, local_width),
        "cfg",
        split_axis=0,
        concat_axis=0,
        tiled=True,
    )
    conditional = paired[0]
    unconditional = paired[1]
    raw = unconditional + guidance_scale * (conditional - unconditional)
    entries = float(SEQ_LEN * D)
    own_square = lax.psum(own_local, ("seq", "tp"))
    raw_square, cond_square = lax.psum(
        (jnp.sum(raw * raw, axis=(1, 2)), jnp.sum(conditional * conditional, axis=(1, 2))),
        ("seq", "tp"),
    )
    state_norm = jnp.sqrt(own_square / entries + norm_eps)
    factor = rescale_share * jnp.sqrt(cond_square / entries + norm_eps) / jnp.sqrt(
        raw_square / entries + norm_eps
    ) + (1.0 - rescale_share)
    guided = (raw * factor[:, None, None]).astype(jnp.bfloat16)
    return (guided, state_norm[None, :], peak_logit[None, :])


CHUNKS = 2


def gather_scalars_kernel(value_ref, total_ref, peak_ref, held, send_sems, recv_sems):
    cfg = lax.axis_index("cfg")
    seq_size, tp_size = lax.axis_size("seq"), lax.axis_size("tp")
    count = seq_size * tp_size
    me = lax.axis_index("seq") * tp_size + lax.axis_index("tp")

    def place(step):
        other = lax.rem(me + step, count)
        return (cfg, other // tp_size, lax.rem(other, tp_size))

    barrier = pltpu.get_barrier_semaphore()
    for step in range(1, count):
        pl.semaphore_signal(
            barrier, inc=1, device_id=place(step), device_id_type=pl.DeviceIdType.MESH
        )
    pl.semaphore_wait(barrier, count - 1)
    copies = []
    for step in range(1, count):
        copy = pltpu.make_async_remote_copy(
            src_ref=value_ref,
            dst_ref=held.at[step],
            send_sem=send_sems.at[step],
            recv_sem=recv_sems.at[step],
            device_id=place(step),
            device_id_type=pl.DeviceIdType.MESH,
        )
        copy.start()
        copies.append(copy)
    total = value_ref[...]
    peak = value_ref[...]
    for step, copy in enumerate(copies):
        copy.wait()
        total = total + held[step + 1]
        peak = jnp.maximum(peak, held[step + 1])
    total_ref[...] = total
    peak_ref[...] = peak


def gather_scalars(values):
    count = lax.axis_size("seq") * lax.axis_size("tp")
    shape = jax.ShapeDtypeStruct((8, 128), jnp.float32)
    return pl.pallas_call(
        gather_scalars_kernel,
        out_shape=(shape, shape),
        in_specs=[pl.BlockSpec(memory_space=pltpu.VMEM)],
        out_specs=(
            pl.BlockSpec(memory_space=pltpu.VMEM),
            pl.BlockSpec(memory_space=pltpu.VMEM),
        ),
        scratch_shapes=[
            pltpu.VMEM((count, 8, 128), jnp.float32),
            pltpu.SemaphoreType.DMA((count,)),
            pltpu.SemaphoreType.DMA((count,)),
        ],
        compiler_params=pltpu.CompilerParams(collective_id=0, has_side_effects=True),
    )(values)


def send_back(summed, seq_size):
    return lax.all_to_all(
        summed.reshape(seq_size, summed.shape[0] // seq_size, summed.shape[1]),
        "seq",
        split_axis=0,
        concat_axis=0,
        tiled=True,
    )


def local_by_request(
    hidden_in, w_qkv, w_mlp, w_attn_out, w_mlp_out, mod_table, qk_gain, timestep, text_len, pos_ids
):
    tokens = hidden_in[0]
    requests, local_len, local_width = tokens.shape
    head_size = qk_gain.shape[1]
    local_inner = w_qkv.shape[2]
    local_heads = local_inner // head_size
    seq_size = lax.axis_size("seq")
    total_len = local_len * seq_size
    half_req = requests // 2
    my_request = lax.axis_index("seq")
    my_copy = lax.axis_index("cfg")
    modulation = lookup_rows(mod_table, timestep)
    own_mod = lax.dynamic_slice_in_dim(modulation, my_request, 1, 0)

    step_in = local_len // CHUNKS
    w_flat = w_qkv.reshape(w_qkv.shape[0], 3 * local_inner)
    pos_mine = lax.all_to_all(pos_ids, "seq", split_axis=0, concat_axis=0, tiled=True)
    modded_parts = []
    for c in range(CHUNKS):
        piece = lax.slice_in_dim(tokens, c * step_in, (c + 1) * step_in, axis=1)
        got = lax.all_to_all(piece, "seq", split_axis=0, concat_axis=0, tiled=True)
        if c == 0:
            got, w_flat = lax.optimization_barrier((got, w_flat))
        rows = got.reshape(seq_size * step_in, local_width)
        full = lax.all_gather(rows, "tp", axis=1, tiled=True)
        modded_parts.append(modulate(full[None], own_mod)[0])
    kept = lax.dynamic_slice_in_dim(tokens, my_copy * half_req, half_req, 0)
    sent = lax.dynamic_slice_in_dim(tokens, (1 - my_copy) * half_req, half_req, 0)
    received = lax.ppermute(sent, "cfg", [(0, 1), (1, 0)])

    positions = (
        jnp.arange(seq_size, dtype=jnp.int32)[None, :, None] * local_len
        + jnp.arange(CHUNKS, dtype=jnp.int32)[:, None, None] * step_in
        + jnp.arange(step_in, dtype=jnp.int32)[None, None, :]
    ).reshape(total_len)
    ids = pos_mine.reshape(seq_size, 3, CHUNKS, step_in)
    ids = jnp.transpose(ids, (1, 2, 0, 3)).reshape(1, 3, total_len)
    cosine, sine_table, swapper = rope_tables(ids, head_size)
    length = lax.dynamic_slice_in_dim(text_len[0], my_request, 1, 0)
    usable = (positions >= TXT) | (positions < length)
    score_scale = head_size ** (-0.5)

    q_parts, k_parts, v_parts, hidden_parts = [], [], [], []
    part_len = seq_size * step_in
    for c in range(CHUNKS):
        projected = jnp.dot(modded_parts[c], w_flat, preferred_element_type=jnp.float32)
        projected = projected.reshape(1, part_len, 3, local_heads, head_size)
        cos_c = lax.slice_in_dim(cosine, c * part_len, (c + 1) * part_len, axis=1)
        sin_c = lax.slice_in_dim(sine_table, c * part_len, (c + 1) * part_len, axis=1)
        q_parts.append(
            rotate(head_norm(projected[:, :, 0], qk_gain[0]), cos_c, sin_c, swapper).astype(
                jnp.bfloat16
            )[0]
        )
        k_parts.append(
            rotate(head_norm(projected[:, :, 1], qk_gain[1]), cos_c, sin_c, swapper).astype(
                jnp.bfloat16
            )[0]
        )
        v_parts.append(projected[0, :, 2].astype(jnp.bfloat16))
        hidden_parts.append(
            jax.nn.gelu(
                jnp.dot(modded_parts[c], w_mlp, preferred_element_type=jnp.float32),
                approximate=True,
            ).astype(jnp.bfloat16)
        )
    keys = jnp.concatenate(k_parts, axis=0)
    values = jnp.concatenate(v_parts, axis=0)
    keys, received = lax.optimization_barrier((keys, received))

    peak = jnp.float32(masked_value)
    own_parts, other_parts = [], []
    partial_out = summed = None
    for c in range(CHUNKS):
        query_rows = q_parts[c]
        if c > 0:
            query_rows, partial_out = lax.optimization_barrier((query_rows, partial_out))
            summed = lax.psum_scatter(partial_out, "tp", scatter_dimension=1, tiled=True)
        scores = (
            jnp.einsum("qhd,khd->hqk", query_rows, keys, preferred_element_type=jnp.float32)
            * score_scale
        )
        scores = jnp.where(usable[None, None, :], scores, masked_value)
        row_peak = jnp.max(scores, axis=-1)
        weights = jnp.where(usable[None, None, :], jnp.exp(scores - row_peak[..., None]), 0.0)
        weight_sum = jnp.sum(weights, axis=-1)
        mixture = jnp.einsum(
            "hqk,khd->qhd", weights.astype(jnp.bfloat16), values, preferred_element_type=jnp.float32
        )
        mixture = mixture / jnp.transpose(weight_sum, (1, 0))[..., None]
        attended = mixture.reshape(part_len, local_inner).astype(jnp.bfloat16)
        peak = jnp.maximum(peak, jnp.max(row_peak))
        if c > 0:
            own_parts.append(send_back(summed, seq_size))
        partial_out = (
            jnp.dot(attended, w_attn_out, preferred_element_type=jnp.float32)
            + jnp.dot(hidden_parts[c], w_mlp_out, preferred_element_type=jnp.float32)
        ).astype(jnp.bfloat16)
    summed = lax.psum_scatter(partial_out, "tp", scatter_dimension=1, tiled=True)
    own_parts.append(send_back(summed, seq_size))
    for back in own_parts:
        other_parts.append(
            lax.all_to_all(
                back.reshape(2, half_req, step_in, local_width),
                "cfg",
                split_axis=0,
                concat_axis=0,
                tiled=True,
            )
        )
    swapped = jnp.stack(
        [jnp.where(my_copy == 0, kept, received), jnp.where(my_copy == 0, received, kept)]
    )
    gate_rows = lax.dynamic_slice_in_dim(
        modulation[:, 2, :], lax.axis_index("tp") * local_width, local_width, 1
    )
    guide_gate = lax.dynamic_slice_in_dim(gate_rows, my_copy * half_req, half_req, 0)
    own_sum = jnp.zeros((requests,), jnp.float32)
    raw_sum = jnp.zeros((half_req,), jnp.float32)
    cond_sum = jnp.zeros((half_req,), jnp.float32)
    raws = []
    for c in range(CHUNKS):
        at = slice(c * step_in, (c + 1) * step_in)
        own_state = tokens[:, at].astype(jnp.float32) + gate_rows[:, None, :] * own_parts[c].astype(
            jnp.float32
        )
        own_sum = own_sum + jnp.sum(own_state * own_state, axis=(1, 2))
        pair = swapped[:, :, at].astype(jnp.float32) + guide_gate[None, :, None, :] * other_parts[
            c
        ].astype(jnp.float32)
        raw = pair[1] + guidance_scale * (pair[0] - pair[1])
        raw_sum = raw_sum + jnp.sum(raw * raw, axis=(1, 2))
        cond_sum = cond_sum + jnp.sum(pair[0] * pair[0], axis=(1, 2))
        raws.append(raw)
    entries = float(SEQ_LEN * D)
    sums = jnp.concatenate([own_sum, raw_sum, cond_sum])
    peaks = jnp.where(jnp.arange(requests) == my_request, peak, masked_value)
    block = jnp.stack([jnp.pad(v, (0, 128 - v.shape[0])) for v in (sums, peaks)])
    total, highest = gather_scalars(jnp.pad(block, ((0, 6), (0, 0))))
    peak_logit = highest[1, :requests]
    own_square = total[0, :requests]
    raw_square = total[0, requests : requests + half_req]
    cond_square = total[0, requests + half_req : 2 * requests]
    state_norm = jnp.sqrt(own_square / entries + norm_eps)
    factor = rescale_share * jnp.sqrt(cond_square / entries + norm_eps) / jnp.sqrt(
        raw_square / entries + norm_eps
    ) + (1.0 - rescale_share)
    guided = (jnp.concatenate(raws, axis=1) * factor[:, None, None]).astype(jnp.bfloat16)
    return (guided, state_norm[None, :], peak_logit[None, :])


def solution(mesh):
    placed = (
        P("cfg", None, "seq", "tp"),
        P(None, None, "tp"),
        P(None, "tp"),
        P("tp", None),
        P("tp", None),
        P(),
        P(),
        P(),
        P("cfg", None),
        P(None, None, "seq"),
    )
    body = local_by_request if mesh.shape["seq"] == REQUESTS else local
    return jax.shard_map(
        body,
        mesh=mesh,
        in_specs=placed,
        out_specs=(P("cfg", "seq", "tp"), P("cfg", None), P("cfg", None)),
        check_vma=False,
    )
```
